128 devices in a mesh: loop: 2 (over z_lo), blk: 64 (over z_hi, x, y, core).
Axes of the slice: x: 4, y: 4, z: 4 (z_hi: 2, z_lo: 2; z = z_hi * 2 + z_lo), core: 2. Of those that a mesh axis runs over, the one named last changes fastest.
Arguments:
- queries: bfloat16 [2, 8192, 4096], P('loop', 'blk'), may hold values from -60 to 60
- keys: bfloat16 [2, 8192, 512], P('loop', 'blk'), may hold values from -60 to 60
- values: bfloat16 [2, 8192, 512], P('loop', 'blk'), may hold values from -6 to 6
- match: int32 [128], P(('loop', 'blk')), may hold values from 0 to 1
- dec_queries: bfloat16 [2, 4096, 4096], P(None, ('loop', 'blk')), may hold values from -60 to 60
- new_keys: bfloat16 [2, 4096, 512], P(None, ('loop', 'blk')), may hold values from -60 to 60
- new_values: bfloat16 [2, 4096, 512], P(None, ('loop', 'blk')), may hold values from -6 to 6
- row_len: int32 [4096], P(('loop', 'blk')), may hold values from 1024 to 8192, as said below
Outputs:
- prompt_out: bfloat16 [2, 8192, 4096], P('loop', 'blk')
- handed_cache: bfloat16 [128, 2, 8192, 512], P(('loop', 'blk'))
- dec_out: bfloat16 [2, 4096, 4096], P(None, ('loop', 'blk'))
The draws below stay inside these ranges and needn't reach their ends.
Inputs may be any that keep to these rules, and one draw needn't show every extreme that they name: `row_len`: the first of each device's 32 requests has 8192.
All inputs are finite; a program needn't handle non-finite values.
Results may differ from the reference program's by a relative error of at most 0.009.
Values may be sent and summed in bfloat16 or wider, within the bound.
No kernel may reach another device: no remote copies, remote signals or barrier semaphores. Data moves between devices by JAX's collectives and lax.ppermute only.
A program may use at most 256 MiB of HBM per device.

```python
import math
import jax
import jax.numpy as jnp
from jax import lax

H = 32
KVH = 4
HD = 128
ROW_DEV = 32
STEPS = 2
GROUP = 8
SEQ = 8192
ROWS = 4096
N_LOOP = 2
DEVICES = 128


def shared_base(key):
    base = jax.random.normal(key, (STEPS, ROWS, KVH, 1, HD), jnp.float32)
    return jnp.clip(base, -4.0, 4.0)


def draw_queries(key, part):
    key = jax.random.fold_in(key, 13)
    query = jnp.clip(jax.random.normal(key, (N_LOOP, SEQ, KVH, GROUP, HD), jnp.float32), -4.0, 4.0)
    return query.reshape(N_LOOP, SEQ, H * HD).astype(jnp.bfloat16)


def draw_keys(key, part):
    key = jax.random.fold_in(key, 17)
    fresh = jnp.clip(jax.random.normal(key, (N_LOOP, SEQ, KVH, 1, HD), jnp.float32), -4.0, 4.0)
    return fresh.reshape(N_LOOP, SEQ, KVH * HD).astype(jnp.bfloat16)


def draw_dec_queries(key, part):
    base = shared_base(key)
    key = jax.random.fold_in(key, 3)
    noise = jnp.clip(jax.random.normal(key, (STEPS, ROWS, KVH, GROUP, HD), jnp.float32), -4.0, 4.0)
    query = 0.8 * base + 0.6 * noise
    return query.reshape(STEPS, ROWS, H * HD).astype(jnp.bfloat16)


def draw_new_keys(key, part):
    base = shared_base(key)
    key = jax.random.fold_in(key, 5)
    noise = jnp.clip(jax.random.normal(key, (STEPS, ROWS, KVH, 1, HD), jnp.float32), -4.0, 4.0)
    fresh = 0.75 * base + 0.5 * noise
    return fresh.reshape(STEPS, ROWS, KVH * HD).astype(jnp.bfloat16)


def draw_row_len(key, part):
    key = jax.random.fold_in(key, 7)
    lens = jax.random.randint(key, (ROWS,), SEQ // 8, SEQ + 1, jnp.int32)
    first = jnp.arange(ROWS, dtype=jnp.int32) % ROW_DEV == 0
    return jnp.where(first, SEQ, lens).astype(jnp.int32)


def plant(values, rng, smallest, largest):
    extent = values.shape
    place = [jax.random.randint(jax.random.fold_in(rng, axis), (), 0, extent[axis]) for axis in range(len(extent))]
    values = values.at[tuple(place)].set(smallest)
    longest = extent.index(max(extent))
    place[longest] = (place[longest] + 1) % extent[longest]
    return values.at[tuple(place)].set(largest)


def block_levels(stream_key, shape, split, least, high):
    level, own = 1.0, jax.random.fold_in(stream_key, 6)
    for axis_at, parts in split:
        heights = jnp.exp(jax.random.uniform(jax.random.fold_in(own, axis_at), (parts,), jnp.float32, least / len(split), high / len(split)))
        level = level * jnp.repeat(heights, shape[axis_at] // parts).reshape([-1 if axis == axis_at else 1 for axis in range(len(shape))])
    return level


def gaussian(rng, shape, scale, bound, pieces=(), kind=jnp.bfloat16):
    factor_of = block_levels(rng, shape, pieces, -0.22, 0.18) if pieces else 1.0
    drawn = jax.random.normal(rng, shape, jnp.float32) * scale * factor_of
    return jnp.minimum(jnp.maximum(drawn, -bound), bound).astype(kind)


def setup_inputs(seed: int = 0) -> dict:
    key_of = jax.random.split(jax.random.key(seed), 9)
    queries = draw_queries(jax.random.fold_in(key_of[8], 71), 0)
    keys = draw_keys(jax.random.fold_in(key_of[8], 71), 0)
    values = gaussian(key_of[2], (N_LOOP, SEQ, KVH * HD), 1.0, 6.0, ((0, 2), (1, 64)))
    match = plant(jax.random.randint(key_of[3], (DEVICES,), 0, N_LOOP), jax.random.fold_in(key_of[3], 1), 0, N_LOOP - 1).astype(jnp.int32)
    dec_queries = draw_dec_queries(jax.random.fold_in(key_of[8], 71), 0)
    new_keys = draw_new_keys(jax.random.fold_in(key_of[8], 71), 0)
    new_values = gaussian(key_of[6], (STEPS, ROWS, KVH * HD), 1.0, 6.0, ((1, 128),))
    row_len = draw_row_len(jax.random.fold_in(key_of[8], 71), 0)
    return dict(queries=queries, keys=keys, values=values, match=match, dec_queries=dec_queries, new_keys=new_keys, new_values=new_values, row_len=row_len)


def prompt_attention(query_all, key_all, value_all):
    qblock = min(256, SEQ)
    scale = 1.0 / math.sqrt(HD)
    kf = key_all.astype(jnp.float32).reshape(SEQ, KVH, HD)
    vf = value_all.astype(jnp.float32).reshape(SEQ, KVH, HD)

    def one_block(index):
        start = (index * qblock).astype(jnp.int32)
        qpart = lax.dynamic_slice_in_dim(query_all, start, qblock, 0)
        qpart = qpart.astype(jnp.float32).reshape(qblock, KVH, GROUP, HD)
        scores = jnp.einsum('tkgd,skd->kgts', qpart, kf) * scale
        allow = jnp.arange(SEQ, dtype=jnp.int32)[None, :] <= (start + jnp.arange(qblock, dtype=jnp.int32))[:, None]
        scores = jnp.where(allow, scores, -1e+30)
        top = lax.optimization_barrier(jnp.max(scores, axis=-1, keepdims=True))
        weights = jnp.where(allow, jnp.exp(scores - top), 0.0)
        total = lax.optimization_barrier(jnp.sum(weights, axis=-1))
        rounded = lax.optimization_barrier(weights.astype(jnp.bfloat16)).astype(jnp.float32)
        acc = jnp.einsum('kgts,skd->kgtd', rounded, vf)
        result = acc / total[..., None]
        return result.transpose(2, 0, 1, 3).reshape(qblock, H * HD).astype(jnp.bfloat16)
    blocks = lax.map(one_block, jnp.arange(SEQ // qblock, dtype=jnp.int32))
    return blocks.reshape(SEQ, H * HD)

def reference(queries, keys, values, match, dec_queries, new_keys, new_values, row_len):
    prompt_out = jnp.stack([prompt_attention(queries[p], keys[p], values[p]) for p in range(N_LOOP)])
    handed_cache = jnp.stack([keys[match], values[match]], axis=1)
    scale = 1.0 / math.sqrt(HD)
    dq = dec_queries.reshape(STEPS, DEVICES, ROW_DEV, H * HD).transpose(1, 0, 2, 3)
    nk = new_keys.reshape(STEPS, DEVICES, ROW_DEV, KVH * HD).transpose(1, 0, 2, 3)
    nv = new_values.reshape(STEPS, DEVICES, ROW_DEV, KVH * HD).transpose(1, 0, 2, 3)
    lens = row_len.reshape(DEVICES, ROW_DEV)

    def one_device(packed):
        qd, kd, vd, lend, prompt = packed
        cache_k = lax.dynamic_index_in_dim(keys, prompt, 0, keepdims=False).astype(jnp.float32).reshape(SEQ, KVH, HD)
        cache_v = lax.dynamic_index_in_dim(values, prompt, 0, keepdims=False).astype(jnp.float32).reshape(SEQ, KVH, HD)
        allow = jnp.arange(SEQ, dtype=jnp.int32)[None, :] < lend[:, None]
        outs = []
        for step in range(STEPS):
            query = qd[step].astype(jnp.float32).reshape(ROW_DEV, KVH, GROUP, HD)
            scores = jnp.einsum('rkgd,skd->rkgs', query, cache_k) * scale
            scores = jnp.where(allow[:, None, None, :], scores, -1e+30)
            fresh_k = kd[:step + 1].astype(jnp.float32).reshape(step + 1, ROW_DEV, KVH, HD)
            fresh_v = vd[:step + 1].astype(jnp.float32).reshape(step + 1, ROW_DEV, KVH, HD)
            fresh = jnp.einsum('rkgd,jrkd->rkgj', query, fresh_k) * scale
            top = jnp.maximum(lax.optimization_barrier(jnp.max(scores, axis=-1)), lax.optimization_barrier(jnp.max(fresh, axis=-1)))
            weights = jnp.where(allow[:, None, None, :], jnp.exp(scores - top[..., None]), 0.0)
            fresh_w = jnp.exp(fresh - top[..., None])
            total = lax.optimization_barrier(jnp.sum(weights, axis=-1)) + lax.optimization_barrier(jnp.sum(fresh_w, axis=-1))
            rounded = lax.optimization_barrier(weights.astype(jnp.bfloat16)).astype(jnp.float32)
            fresh_r = lax.optimization_barrier(fresh_w.astype(jnp.bfloat16)).astype(jnp.float32)
            acc = jnp.einsum('rkgs,skd->rkgd', rounded, cache_v) + jnp.einsum('rkgj,jrkd->rkgd', fresh_r, fresh_v)
            outs.append((acc / total[..., None]).reshape(ROW_DEV, H * HD).astype(jnp.bfloat16))
        return jnp.stack(outs)
    decoded = lax.map(one_device, (dq, nk, nv, lens, match))
    dec_out = decoded.transpose(1, 0, 2, 3).reshape(STEPS, ROWS, H * HD)
    return (prompt_out, handed_cache, dec_out)
```

```python
import functools
import math

import jax
import jax.numpy as jnp
from jax import lax
from jax.experimental import pallas as pl
from jax.experimental.pallas import tpu as pltpu
from jax.sharding import PartitionSpec as P

HD = 128
TOK = 128
SEG = 48
ROWS = TOK + SEG
AX = ("loop", "blk")
ROTS = ("xyz", "yzx", "zxy")
LEAD = (0, 1, 0)
SCALE = 1.0 / math.sqrt(HD)
LOG2 = math.log2(math.e) * SCALE
NEG = -1e30
BIG = 1 << 30
LIMIT = 100.0


def index(x, y, z, c):
    return (z % 2) * 64 + (((z // 2) * 4 + x) * 4 + y) * 2 + c


def moved(value, dim, rule):
    at = "xyz".index(dim)
    route = []
    for flat in range(128):
        c, y, x, z = flat % 2, flat // 2 % 4, flat // 8 % 4, flat // 32
        there = [x, y, z]
        there[at] = rule(there[at], c) % 4
        route.append((index(x, y, z, c), index(*there, c)))
    return lax.ppermute(value, AX, route)


def swapped(value):
    return lax.ppermute(value, AX, [(i, i ^ 1) for i in range(128)])


def tied(values):
    return list(lax.optimization_barrier(tuple(values)))


def dot_nt(a, b):
    return lax.dot_general(a, b, (((1,), (1,)), ((), ())), preferred_element_type=jnp.float32)


def dot_nn(a, b):
    return lax.dot_general(a, b, (((1,), (0,)), ((), ())), preferred_element_type=jnp.float32)


def lane_sums(w):
    total = w[:, :128]
    for at in range(128, w.shape[1], 128):
        total = total + w[:, at : at + 128]
    return total


def positions(bases, n, live):
    it = lax.broadcasted_iota(jnp.int32, (1, len(bases) * n), 1)
    pos = it + bases[0]
    inside = it
    for s in range(1, len(bases)):
        pos = jnp.where(it >= s * n, it + (bases[s] - s * n), pos)
        inside = jnp.where(it >= s * n, it - s * n, inside)
    return jnp.where(inside < live, pos, BIG)


def stage_kernel(stage, meta, lens, q, dq, o0, o1, o2, s0, s1, s2, *rest):
    last = stage == 3
    accs_in, rest = rest[:4], rest[5:]
    if last:
        (pout, dout, handed, mx), rest = rest[:4], rest[4:]
        accs_out = None
    else:
        accs_out, handed, mx, rest = rest[:4], rest[4], rest[5], rest[6:]
    buf, sp, sl, dp, dl, load_sem, acc_sem, out_sem, hand_sem = rest
    accs = (sp, sl, dp, dl)
    px, py, pz, core, match = meta[0], meta[1], meta[2], meta[3], meta[4]
    mine = (((pz >> 1) * 4 + px) * 4 + py) * 2 + core
    same = match == (pz & 1)
    odd = stage % 2 == 1

    loads = [
        pltpu.make_async_copy(src, buf.at[r, side], load_sem.at[r, side])
        for r, pair in enumerate(((o0, s0), (o1, s1), (o2, s2)))
        for side, src in enumerate(pair)
    ]
    for copy in loads:
        copy.start()
    first = 2 if stage == 0 else 0
    acc_loads = [
        pltpu.make_async_copy(accs_in[i], accs[i], acc_sem.at[i]) for i in range(first, 4)
    ]
    for copy in acc_loads:
        copy.start()
    if stage == 0:
        sp[...] = jnp.zeros_like(sp)
        sl[...] = jnp.zeros_like(sl)
    for copy in acc_loads:
        copy.wait()
    for copy in loads:
        copy.wait()

    def place(r, side, lead, inner):
        cs = core if side == 0 else 1 - core

        def offset(i):
            return jnp.where(
                i == 0, 0, jnp.where(i == 3, 2, jnp.where(i == 1, 1 + 2 * cs, 3 - 2 * cs))
            )

        turn = stage * (2 * cs - 1)
        el, ei = offset(lead), offset(inner)
        x = jnp.where(r == 0, px ^ el, jnp.where(r == 1, (px + turn) & 3, px ^ ei))
        y = jnp.where(r == 2, (py + turn) & 3, py ^ ei)
        z = jnp.where(r == 0, (pz + turn) & 3, pz ^ el)
        return (((z >> 1) * 4 + x) * 4 + y) * 2 + cs

    def facing(lead):
        return jnp.where(lead == 1, 2, jnp.where(lead == 2, 1, lead))

    def lead_of(item, own):
        r = jnp.where(item < 2, 1, jnp.where(item < 4, 2, 0))
        near = jnp.where(item % 2 == 0, 0, 3)
        far = 1 + item % 2
        lead = jnp.where(item >= 4, item - 4, jnp.where(own, near, far))
        return r, lead

    def hand(r, lead, act):
        live = min(SEG, TOK - SEG * r)
        for side in range(2):
            at = lead if side == 0 else facing(lead)
            for inner in range(4):
                row = place(r, side, at, inner) * TOK
                for half in range(2):
                    lanes = pl.ds(half * HD, HD)
                    for lo, n, to, head in ((0, TOK, 0, r), (TOK, live, SEG * r, 3)):
                        act(
                            pltpu.make_async_copy(
                                buf.at[r, side, at, inner, pl.ds(lo, n), lanes],
                                handed.at[
                                    half,
                                    pl.ds(pl.multiple_of(row + to, 16), n),
                                    pl.ds(head * HD, HD),
                                ],
                                hand_sem,
                            )
                        )

    def hand_all(act):
        for r in (1, 2):

            def some(i, _):
                hand(r, jnp.where(same, i * 3, 1 + i), act)
                return 0

            lax.fori_loop(0, 2, some, 0)

        @pl.when(jnp.logical_xor(same, odd))
        def _():
            def some(i, _):
                hand(0, i, act)
                return 0

            lax.fori_loop(0, 4, some, 0)

    hand_all(lambda copy: copy.start())

    high = buf[2, 0, :, :, TOK + 32 : TOK + 48, :].reshape(16, 16, 256)
    other = buf[2, 1, :, :, TOK + 32 : TOK + 48, :].reshape(16, 16, 256)
    mx[...] = jnp.max(jnp.maximum(high, other).astype(jnp.float32), axis=0)

    def main_tile(item, own):
        r, lead = lead_of(item, own)
        keys, bases = [], []
        for side in range(2):
            at = lead if side == 0 else facing(lead)
            keys.append(buf[r, side, at, :, 0:TOK, :].reshape(4 * TOK, 256))
            bases += [place(r, side, at, inner) * TOK for inner in range(4)]
        return r, jnp.concatenate(keys, 0), bases, positions(bases, TOK, TOK)

    def third_tile(item, own):
        r = jnp.where(item == 0, 1, jnp.where(item == 1, 2, 0))
        keys, bases = [], []
        for part in range(2):
            lead = jnp.where(
                item >= 2, (item - 2) * 2 + part, jnp.where(own, 3 * part, 1 + part)
            )
            for side in range(2):
                at = lead if side == 0 else facing(lead)
                keys.append(buf[r, side, at, :, TOK:ROWS, :].reshape(4 * SEG, 256))
                bases += [
                    place(r, side, at, inner) * TOK + r * SEG for inner in range(4)
                ]
        live = jnp.where(r == 2, TOK - 2 * SEG, SEG)
        return 3, jnp.concatenate(keys, 0), bases, positions(bases, SEG, live)

    def lowest(bases):
        return functools.reduce(jnp.minimum, bases)

    def prompt_tile(tile, item):
        head, kv, bases, pos = tile(item, True)

        @pl.when(lowest(bases) < mine * TOK)
        def _():
            bias = jnp.where(pos < mine * TOK, 0.0, NEG)
            k, v = kv[:, :HD], kv[:, HD:]
            for chunk in range(4):
                rows = slice(chunk * 256, chunk * 256 + 256)
                parts = []
                for g in range(2 * chunk, 2 * chunk + 2):
                    lane = pl.multiple_of((head * 8 + g) * HD, HD)
                    parts.append(q[:, pl.ds(lane, HD)])
                w = jnp.exp2(dot_nt(jnp.concatenate(parts, 0), k) * LOG2 + bias)
                sl[head, rows, :] += lane_sums(w)
                sp[head, rows, :] += dot_nn(w.astype(jnp.bfloat16), v)

    def decode_tile(tile, item):
        head, kv, bases, pos = tile(item, same)
        k, v = kv[:, :HD], kv[:, HD:]
        for chunk in range(2):
            rows = slice(chunk * 256, chunk * 256 + 256)
            parts = []
            for g in range(4 * chunk, 4 * chunk + 4):
                lane = pl.multiple_of((head * 8 + g) * HD, HD)
                parts.append(dq[:, pl.ds(lane, HD)])
            limit = jnp.concatenate([lens[:, 0:1]] * 4, 0)
            s = dot_nt(jnp.concatenate(parts, 0), k) * LOG2
            w = jnp.exp2(jnp.where(pos < limit, s, NEG))
            dl[head, rows, :] += lane_sums(w)
            dp[head, rows, :] += dot_nn(w.astype(jnp.bfloat16), v)

    if stage == 0:
        row = lax.broadcasted_iota(jnp.int32, (256, TOK), 0) % TOK
        col = lax.broadcasted_iota(jnp.int32, (256, TOK), 1)
        for head in range(4):
            if head < 3:
                kv = buf[head, 0, 0, 0, 0:TOK, :]
            else:
                kv = jnp.concatenate(
                    [
                        buf[r, 0, 0, 0, TOK : TOK + min(SEG, TOK - SEG * r), :]
                        for r in range(3)
                    ],
                    0,
                )
            k, v = kv[:, :HD], kv[:, HD:]
            for chunk in range(4):
                rows = slice(chunk * 256, chunk * 256 + 256)
                parts = [
                    q[:, (head * 8 + g) * HD : (head * 8 + g + 1) * HD]
                    for g in (2 * chunk, 2 * chunk + 1)
                ]
                s = dot_nt(jnp.concatenate(parts, 0), k) * LOG2
                w = jnp.exp2(jnp.where(col <= row, s, NEG))
                sl[head, rows, :] += lane_sums(w)
                sp[head, rows, :] += dot_nn(w.astype(jnp.bfloat16), v)

    def loop(count, work, tile):
        def one(i, _):
            work(tile, i)
            return 0

        lax.fori_loop(0, count, one, 0)

    spread = jnp.where(jnp.logical_xor(same, odd), 1, 0)
    loop(4 if odd else 8, prompt_tile, main_tile)
    loop(2 if odd else 4, prompt_tile, third_tile)
    loop(4 + 4 * spread, decode_tile, main_tile)
    loop(2 + 2 * spread, decode_tile, third_tile)

    if last:
        for head in range(4):
            for g in range(8):
                lanes = slice((head * 8 + g) * HD, (head * 8 + g + 1) * HD)
                rows = slice(g * TOK, (g + 1) * TOK)
                total = jnp.sum(sl[head, rows, :], axis=1, keepdims=True)
                pout[:, lanes] = (sp[head, rows, :] / total).astype(jnp.bfloat16)
                rows = slice(g * 64, (g + 1) * 64)
                total = jnp.sum(dl[head, rows, :], axis=1, keepdims=True)
                dout[:, lanes] = (dp[head, rows, :] / total).astype(jnp.bfloat16)
    else:
        stores = [
            pltpu.make_async_copy(accs[i], accs_out[i], out_sem.at[i]) for i in range(4)
        ]
        for copy in stores:
            copy.start()
        for copy in stores:
            copy.wait()
    hand_all(lambda copy: copy.wait())


def run_stage(stage, meta, lens, q, dq, own, sib, accs, handed):
    anywhere = pl.BlockSpec(memory_space=pl.ANY)
    vmem = pl.BlockSpec(memory_space=pltpu.VMEM)
    acc_shapes = [jax.ShapeDtypeStruct(a.shape, a.dtype) for a in accs]
    handed_shape = jax.ShapeDtypeStruct((2, 8192, 512), jnp.bfloat16)
    mx_shape = jax.ShapeDtypeStruct((16, 256), jnp.float32)
    if stage == 3:
        outs = [
            jax.ShapeDtypeStruct(q.shape, jnp.bfloat16),
            jax.ShapeDtypeStruct(dq.shape, jnp.bfloat16),
            handed_shape,
            mx_shape,
        ]
        specs = [vmem, vmem, anywhere, vmem]
        alias = {14: 2}
    else:
        outs = [*acc_shapes, handed_shape, mx_shape]
        specs = [anywhere] * 5 + [vmem]
        alias = {10: 0, 11: 1, 12: 2, 13: 3, 14: 4}
    units = (2 * 64 if stage % 2 == 0 else 2 * 32) * 128
    return pl.pallas_call(
        functools.partial(stage_kernel, stage),
        out_shape=outs,
        in_specs=[pl.BlockSpec(memory_space=pltpu.SMEM), vmem, vmem, vmem] + [anywhere] * 11,
        out_specs=specs,
        input_output_aliases=alias,
        scratch_shapes=[
            pltpu.VMEM((3, 2, 4, 4, ROWS, 256), jnp.bfloat16),
            pltpu.VMEM((4, 1024, HD), jnp.float32),
            pltpu.VMEM((4, 1024, HD), jnp.float32),
            pltpu.VMEM((4, 512, HD), jnp.float32),
            pltpu.VMEM((4, 512, HD), jnp.float32),
            pltpu.SemaphoreType.DMA((3, 2)),
            pltpu.SemaphoreType.DMA((4,)),
            pltpu.SemaphoreType.DMA((4,)),
            pltpu.SemaphoreType.DMA,
        ],
        compiler_params=pltpu.CompilerParams(vmem_limit_bytes=40 * 2**20),
        cost_estimate=pl.CostEstimate(
            flops=units * 1024 * 512, bytes_accessed=30 << 20, transcendentals=units * 1024
        ),
        name=f"stage{stage}",
    )(meta, lens, q, dq, *own, *sib, *accs, handed)


def fresh_part(dec_queries, new_keys, new_values):
    steps, rows = dec_queries.shape[:2]
    dq = dec_queries.reshape(steps, rows, 4, 8, HD).astype(jnp.float32)
    nk = new_keys.reshape(steps, rows, 4, 1, HD).astype(jnp.float32)
    nv = new_values.reshape(steps, rows, 4, 1, HD).astype(jnp.float32)
    acc = total = 0.0
    for j in range(steps):
        s = jnp.sum(dq * nk[j], axis=-1, keepdims=True) * LOG2
        allow = (jnp.arange(steps) >= j).reshape(steps, 1, 1, 1, 1)
        w = jnp.exp2(jnp.where(allow, s, NEG))
        total = total + w
        acc = acc + w.astype(jnp.bfloat16).astype(jnp.float32) * nv[j]
    total = jnp.broadcast_to(total / HD, acc.shape)

    def rowwise(v):
        return v.transpose(2, 3, 0, 1, 4).reshape(4, 8 * steps * rows, HD)

    return rowwise(acc), rowwise(total)


def careful(queries, keys, values, handed, dec_queries, new_keys, new_values, row_len):
    place = lax.axis_index("blk")
    tok, block = TOK, 512
    all_k = lax.all_gather(keys[0], "blk", tiled=True).reshape(-1, 4, HD)
    all_v = lax.all_gather(values[0], "blk", tiled=True).reshape(-1, 4, HD)
    seq = all_k.shape[0]

    def attend(query, cache_k, cache_v, limit, state):
        def turn(i, state):
            big, total, acc = state
            part_k = lax.dynamic_slice_in_dim(cache_k, i * block, block, 0)
            part_v = lax.dynamic_slice_in_dim(cache_v, i * block, block, 0)
            s = jnp.einsum("tkgd,skd->kgts", query, part_k, preferred_element_type=jnp.float32)
            s = s * SCALE
            allow = (i * block + jnp.arange(block))[None, :] < limit[:, None]
            s = jnp.where(allow, s, NEG)
            top = jnp.maximum(big, jnp.max(s, axis=-1))
            w = jnp.where(allow, jnp.exp(s - top[..., None]), 0.0)
            shrink = jnp.exp(big - top)
            total = total * shrink + jnp.sum(w, axis=-1)
            acc = acc * shrink[..., None] + jnp.einsum(
                "kgts,skd->kgtd",
                w.astype(jnp.bfloat16),
                part_v,
                preferred_element_type=jnp.float32,
            )
            return top, total, acc

        return lax.fori_loop(0, seq // block, turn, state)

    def finish(state, rows):
        out = state[2] / state[1][..., None]
        return out.transpose(2, 0, 1, 3).reshape(rows, 4096).astype(jnp.bfloat16)

    state = (
        jnp.full((4, 8, tok), NEG, jnp.float32),
        jnp.zeros((4, 8, tok), jnp.float32),
        jnp.zeros((4, 8, tok, HD), jnp.float32),
    )
    limit = place * tok + jnp.arange(tok) + 1
    state = attend(queries[0].reshape(tok, 4, 8, HD), all_k, all_v, limit, state)
    prompt_out = finish(state, tok)

    steps, rows = dec_queries.shape[:2]
    cache_k = handed[0].reshape(seq, 4, HD)
    cache_v = handed[1].reshape(seq, 4, HD)
    outs = []
    for step in range(steps):
        dquery = dec_queries[step].reshape(rows, 4, 8, HD)
        nk = new_keys[: step + 1].reshape(step + 1, rows, 4, HD)
        nv = new_values[: step + 1].reshape(step + 1, rows, 4, HD)
        s = jnp.einsum("rkgd,jrkd->kgrj", dquery, nk, preferred_element_type=jnp.float32) * SCALE
        top = jnp.max(s, axis=-1)
        w = jnp.exp(s - top[..., None])
        acc = jnp.einsum(
            "kgrj,jrkd->kgrd", w.astype(jnp.bfloat16), nv, preferred_element_type=jnp.float32
        )
        state = attend(dquery, cache_k, cache_v, row_len, (top, jnp.sum(w, axis=-1), acc))
        outs.append(finish(state, rows))
    return prompt_out, jnp.stack(outs)


def longest(value):
    parts = value.astype(jnp.float32).reshape(-1, HD)
    return jnp.sqrt(jnp.max(jnp.sum(parts * parts, axis=-1)))


def body(queries, keys, values, match, dec_queries, new_keys, new_values, row_len):
    flat = lax.axis_index("loop") * 64 + lax.axis_index("blk")
    core, y, x = flat % 2, flat // 2 % 4, flat // 8 % 4
    z = flat // 32 % 2 * 2 + flat // 64
    meta = jnp.stack([x, y, z, core, match[0], 0, 0, 0]).astype(jnp.int32)

    high_k = jnp.maximum(longest(keys), longest(new_keys)) * 1.01
    high_q = jnp.maximum(longest(queries), longest(dec_queries)) * 1.01
    spare = jnp.concatenate(
        [jnp.full((16, HD), high_k), jnp.full((16, HD), high_q)], axis=1
    ).astype(jnp.bfloat16)
    k, v = keys[0], values[0]

    def packed(lo, hi, head):
        lanes = slice(head * HD, (head + 1) * HD)
        return jnp.concatenate([k[lo:hi, lanes], v[lo:hi, lanes]], axis=1)

    pieces = []
    for r in range(3):
        rows = [packed(0, TOK, r), packed(SEG * r, min(SEG * (r + 1), TOK), 3)]
        if r == 2:
            rows.append(spare)
        pieces.append(jnp.concatenate(rows, 0)[None, None])

    pieces = tied(pieces)
    for phase in range(2):
        for step in range(2):
            got = tied(
                [
                    moved(p, rot[phase], lambda a, c: a ^ (1 if step == c else 3))
                    for p, rot in zip(pieces, ROTS)
                ]
            )
            axes = [lead if phase == 0 else 1 - lead for lead in LEAD]
            pieces = tied(
                [jnp.concatenate([p, g], a) for p, g, a in zip(pieces, got, axes)]
            )

    lens = jnp.broadcast_to(jnp.tile(row_len, 2)[:, None], (64, HD)).astype(jnp.int32)
    q, dq = queries[0], dec_queries.reshape(64, 4096)
    dacc, dtotal = fresh_part(dec_queries, new_keys, new_values)
    nothing = jnp.zeros((4, 1024, HD), jnp.float32)
    accs = [nothing, nothing, dacc, dtotal]
    handed = jnp.zeros((2, 8192, 512), jnp.bfloat16)
    high = []
    for stage in range(4):
        sib = [swapped(p) for p in pieces]
        if stage < 3:
            onward = [
                moved(p, rot[2], lambda a, c: a + 1 - 2 * c) for p, rot in zip(pieces, ROTS)
            ]
        res = run_stage(stage, meta, lens, q, dq, pieces, sib, accs, handed)
        if stage < 3:
            accs, handed, mx = res[:4], res[4], res[5]
            pieces = onward
        else:
            prompt_out, dec_out, handed, mx = res
        high.append(mx)
    high = functools.reduce(jnp.maximum, high)
    bound = jnp.max(high[:, :HD]) * jnp.max(high[:, HD:]) * LOG2
    prompt_out, dec_out = lax.cond(
        bound < LIMIT,
        lambda: (prompt_out, dec_out.reshape(dec_queries.shape)),
        lambda: careful(
            queries, keys, values, handed, dec_queries, new_keys, new_values, row_len
        ),
    )
    return prompt_out[None], handed[None], dec_out


def solution(mesh):
    in_specs = (
        P("loop", "blk", None),
        P("loop", "blk", None),
        P("loop", "blk", None),
        P(("loop", "blk")),
        P(None, ("loop", "blk"), None),
        P(None, ("loop", "blk"), None),
        P(None, ("loop", "blk"), None),
        P(("loop", "blk")),
    )
    out_specs = (
        P("loop", "blk", None),
        P(("loop", "blk"), None, None, None),
        P(None, ("loop", "blk"), None),
    )
    return jax.shard_map(body, mesh=mesh, in_specs=in_specs, out_specs=out_specs, check_vma=False)
```

```python
import functools
import math

import jax
import jax.numpy as jnp
from jax import lax
from jax.experimental import pallas as pl
from jax.experimental.pallas import tpu as pltpu
from jax.sharding import PartitionSpec as P

HD = 128
TOK = 128
SEG = 48
ROWS = TOK + SEG
AX = ("loop", "blk")
ROTS = ("xyz", "yzx", "zxy")
LEAD = (0, 1, 0)
SCALE = 1.0 / math.sqrt(HD)
LOG2 = math.log2(math.e) * SCALE
NEG = -1e30
BIG = 1 << 30
LIMIT = 100.0
VMEM = 48 * 2**20


def index(x, y, z, c):
    return (z % 2) * 64 + (((z // 2) * 4 + x) * 4 + y) * 2 + c


def moved(value, dim, rule):
    at = "xyz".index(dim)
    route = []
    for flat in range(128):
        c, y, x, z = flat % 2, flat // 2 % 4, flat // 8 % 4, flat // 32
        there = [x, y, z]
        there[at] = rule(there[at], c) % 4
        route.append((index(x, y, z, c), index(*there, c)))
    return lax.ppermute(value, AX, route)


def swapped(value):
    return lax.ppermute(value, AX, [(i, i ^ 1) for i in range(128)])


def tied(values):
    return list(lax.optimization_barrier(tuple(values)))


def dot_nt(a, b):
    return lax.dot_general(a, b, (((1,), (1,)), ((), ())), preferred_element_type=jnp.float32)


def dot_nn(a, b):
    return lax.dot_general(a, b, (((1,), (0,)), ((), ())), preferred_element_type=jnp.float32)


def lane_sums(w):
    total = w[:, :128]
    for at in range(128, w.shape[1], 128):
        total = total + w[:, at : at + 128]
    return total


def positions(bases, n, live):
    it = lax.broadcasted_iota(jnp.int32, (1, len(bases) * n), 1)
    pos = it + bases[0]
    inside = it
    for s in range(1, len(bases)):
        pos = jnp.where(it >= s * n, it + (bases[s] - s * n), pos)
        inside = jnp.where(it >= s * n, it - s * n, inside)
    return jnp.where(inside < live, pos, BIG)


def pack_kernel(keys, values, q, dq, nk, *pieces):
    ones = jnp.ones((HD, HD), jnp.bfloat16)

    def squares(ref):
        best = jnp.zeros((1, HD), jnp.float32)
        for at in range(0, ref.shape[1], HD):
            part = ref[:, at : at + HD].astype(jnp.float32)
            total = dot_nn((part * part).astype(jnp.bfloat16), ones)
            best = jnp.maximum(best, jnp.max(total, axis=0, keepdims=True))
        return best

    for r, piece in enumerate(pieces):
        live = min(SEG, TOK - SEG * r)
        for half, ref in enumerate((keys, values)):
            lanes = slice(half * HD, (half + 1) * HD)
            piece[0:TOK, lanes] = ref[:, r * HD : (r + 1) * HD]
            piece[TOK : TOK + live, lanes] = ref[SEG * r : SEG * r + live, 3 * HD : 4 * HD]
    for half, best in enumerate(
        (jnp.maximum(squares(keys), squares(nk)), jnp.maximum(squares(q), squares(dq)))
    ):
        bound = jnp.broadcast_to(jnp.sqrt(best) * 1.02, (16, HD))
        pieces[2][TOK + 32 : ROWS, half * HD : (half + 1) * HD] = bound.astype(jnp.bfloat16)


def pack(keys, values, q, dq, nk):
    vmem = pl.BlockSpec(memory_space=pltpu.VMEM)
    return pl.pallas_call(
        pack_kernel,
        out_shape=[jax.ShapeDtypeStruct((ROWS, 256), jnp.bfloat16)] * 3,
        in_specs=[vmem] * 5,
        out_specs=[vmem] * 3,
        compiler_params=pltpu.CompilerParams(vmem_limit_bytes=16 * 2**20),
        name="pack",
    )(keys, values, q, dq, nk)


def stage_kernel(t, meta, lens, q, dq, *rest):
    sides = [side for side, on in enumerate((t < 4, t > 0)) if on]
    first, last = t == 0, t == 4
    count = 3 * len(sides)
    sources, rest = rest[:count], rest[count:]
    if first:
        (nk, nv), accs_in, rest = rest[:2], (), rest[2:]
    else:
        accs_in, rest = rest[:4], rest[5:]
    if last:
        (pout, dout, handed, mx), rest = rest[:4], rest[4:]
    else:
        accs_out, handed, mx, rest = rest[:4], rest[4], rest[5], rest[6:]
    buf, spare, sp, sl, dp, dl, load_sem, spare_sem, acc_sem, out_sem, hand_sem = rest
    accs = (sp, sl, dp, dl)
    px, py, pz, core, match = meta[0], meta[1], meta[2], meta[3], meta[4]
    mine = (((pz >> 1) * 4 + px) * 4 + py) * 2 + core
    same = match == (pz & 1)

    near = t % 2
    active = jnp.where(same, near, 1 - near)

    def load(r, side, part):
        source = sources[3 * sides.index(side) + r]
        if part is None:
            return pltpu.make_async_copy(source, buf.at[r, side], load_sem.at[r, side, 0])
        lead, n = ((0, 1), (3, 1), (1, 2))[part]
        span = pl.ds(lead, n)
        return pltpu.make_async_copy(
            source.at[span], buf.at[r, side, span], load_sem.at[r, side, part]
        )

    acc_loads = {
        (head, i): pltpu.make_async_copy(
            accs_in[i].at[head], accs[i].at[head], acc_sem.at[head, i]
        )
        for head in (1, 2, 0, 3)
        for i in range(0 if first else 4)
    }
    needed = {1: [], 2: [], 0: []}
    for r in (1, 2):
        needed[r] = [load(r, side, part) for part in range(2) for side in sides]
    if near in sides:
        needed[0] = [load(0, near, None)]
    others = [load(r, side, 2) for r in (1, 2) for side in sides]
    if 1 - near in sides:
        others.append(load(0, 1 - near, None))
    for r in (1, 2, 0):
        for copy in needed[r]:
            copy.start()
        if not first:
            for i in range(2):
                acc_loads[r, i].start()
    if not first:
        for i in range(2):
            acc_loads[3, i].start()

    @pl.when(jnp.logical_not(same))
    def _():
        for copy in others:
            copy.start()

    spares = [
        pltpu.make_async_copy(
            sources[3 * sides.index(side) + 2].at[:, :, pl.ds(TOK + 32, 16), :],
            spare.at[side],
            spare_sem.at[side],
        )
        for side in sides
    ]
    if not first:
        for head in (1, 2, 0, 3):
            for i in range(2, 4):
                acc_loads[head, i].start()
    for copy in spares:
        copy.start()
    if first:
        sp[...] = jnp.zeros_like(sp)
        sl[...] = jnp.zeros_like(sl)

    def sided(side):
        if isinstance(side, int):
            return (core, t) if side == 0 else (1 - core, t - 1)
        return jnp.where(side == 0, core, 1 - core), jnp.where(side == 0, t, t - 1)

    def place(r, side, lead, inner):
        cs, stage = sided(side)

        def offset(i):
            return jnp.where(
                i == 0, 0, jnp.where(i == 3, 2, jnp.where(i == 1, 1 + 2 * cs, 3 - 2 * cs))
            )

        turn = stage * (2 * cs - 1)
        el, ei = offset(lead), offset(inner)
        x = jnp.where(r == 0, px ^ el, jnp.where(r == 1, (px + turn) & 3, px ^ ei))
        y = jnp.where(r == 2, (py + turn) & 3, py ^ ei)
        z = jnp.where(r == 0, (pz + turn) & 3, pz ^ el)
        return (((z >> 1) * 4 + x) * 4 + y) * 2 + cs

    def facing(lead):
        return jnp.where(lead == 1, 2, jnp.where(lead == 2, 1, lead))

    def led(side, i, own):
        far = 1 + i if side == 0 else 2 - i
        return jnp.where(own, 3 * i, far)

    def hand(r, act):
        live = min(SEG, TOK - SEG * r)

        def slots(side, lead):
            for inner in range(4):
                row = place(r, side, lead, inner) * TOK
                for half in range(2):
                    for lo, n, to, head in ((0, TOK, 0, r), (TOK, live, SEG * r, 3)):
                        act(
                            pltpu.make_async_copy(
                                buf.at[r, side, lead, inner, pl.ds(lo, n), pl.ds(half * HD, HD)],
                                handed.at[
                                    half,
                                    pl.ds(pl.multiple_of(row + to, 16), n),
                                    pl.ds(head * HD, HD),
                                ],
                                hand_sem,
                            )
                        )

        if r == 0:

            def some(i, _):
                slots(active, i)
                return 0

            @pl.when(usable)
            def _():
                lax.fori_loop(0, 4, some, 0)

        else:

            def some(i, _):
                for side in sides:
                    slots(side, led(side, i, same))
                return 0

            lax.fori_loop(0, 2, some, 0)

    usable = True if len(sides) == 2 else active == sides[0]
    prompt_usable = len(sides) == 2 or near == sides[0]

    def gathered(r, groups, lo, n, base, live):
        keys, bases = [], []
        for side, lead in groups:
            keys.append(buf[r, side, lead, :, lo : lo + n, :].reshape(4 * n, 256))
            bases += [place(r, side, lead, inner) * TOK + base for inner in range(4)]
        return jnp.concatenate(keys, 0), bases, n, live

    def groups_of(r, i, own):
        if r == 0:
            side = near if own is True else active
            return [(side, 2 * i), (side, 2 * i + 1)]
        if len(sides) == 2:
            return [(side, led(side, i, own)) for side in sides]
        return [(sides[0], led(sides[0], j, own)) for j in range(2)]

    def main_tile(r, i, own):
        return gathered(r, groups_of(r, i, own), 0, TOK, 0, TOK)

    def third_tile(r, i, own):
        if r == 0:
            side = near if own is True else active
            groups = [(side, j) for j in range(4)]
        else:
            groups = [(side, led(side, j, own)) for j in range(2) for side in sides]
        return gathered(r, groups, TOK, SEG, SEG * r, min(SEG, TOK - SEG * r))

    def queries_of(head):
        return jnp.concatenate(
            [q[:, (head * 8 + g) * HD : (head * 8 + g + 1) * HD] for g in range(8)], 0
        )

    def prompt_add(head, s, v):
        w = jnp.exp2(s)
        sl[head] += jnp.sum(w.reshape(-1, 8, 1024), axis=0)
        sp[head] += dot_nn(jnp.transpose(v), w.astype(jnp.bfloat16))

    def prompt_tile(head, kv, bases, n, live):
        @pl.when(functools.reduce(jnp.minimum, bases) < mine * TOK)
        def _():
            row = lax.broadcasted_iota(jnp.int32, (n, HD), 0)
            lane = lax.broadcasted_iota(jnp.int32, (n, HD), 1)
            hidden = jnp.concatenate(
                [
                    jnp.where(
                        (lane == 0) & ((row >= live) | (base >= mine * TOK)), NEG, 0.0
                    ).astype(jnp.bfloat16)
                    for base in bases
                ],
                0,
            )
            unit = lax.broadcasted_iota(jnp.int32, (1024, HD), 1) == 0
            qs = jnp.concatenate(
                [queries_of(head), unit.astype(jnp.float32).astype(jnp.bfloat16)], 1
            )
            ks = jnp.concatenate([kv[:, :HD], hidden], 1)
            prompt_add(head, dot_nt(ks, qs) * LOG2, kv[:, HD:])

    def decode_tile(head, kv, bases, n, live):
        k, v = kv[:, :HD], kv[:, HD:]
        pos = positions(bases, n, live)
        limit = jnp.concatenate([lens[:, 0:1]] * 4, 0)
        for chunk in range(2):
            rows = slice(chunk * 256, chunk * 256 + 256)
            at = head * 8 + 4 * chunk
            part = [dq[:, g * HD : (g + 1) * HD] for g in range(at, at + 4)]
            s = dot_nt(jnp.concatenate(part, 0), k) * LOG2
            w = jnp.exp2(jnp.where(pos < limit, s, NEG))
            dl[head, rows, :] += lane_sums(w)
            dp[head, rows, :] += dot_nn(w.astype(jnp.bfloat16), v)

    def own_block(head):
        row = lax.broadcasted_iota(jnp.int32, (TOK, 1024), 0)
        col = lax.broadcasted_iota(jnp.int32, (TOK, 1024), 1) % TOK
        if head < 3:
            kv = buf[head, 0, 0, 0, 0:TOK, :]
        else:
            kv = jnp.concatenate(
                [
                    buf[r, 0, 0, 0, TOK : TOK + min(SEG, TOK - SEG * r), :]
                    for r in range(3)
                ],
                0,
            )
        s = dot_nt(kv[:, :HD], queries_of(head)) * LOG2
        prompt_add(head, jnp.where(row <= col, s, NEG), kv[:, HD:])

    def fresh(head):
        lanes = slice(head * HD, (head + 1) * HD)
        step = lax.broadcasted_iota(jnp.int32, (64, 1), 0) >= 32
        for g in range(8):
            at = (head * 8 + g) * HD
            query = dq[:, at : at + HD].astype(jnp.float32)
            acc = total = 0.0
            for j in range(2):
                rows = slice(32 * j, 32 * j + 32)
                key = jnp.concatenate([nk[rows, lanes]] * 2, 0).astype(jnp.float32)
                value = jnp.concatenate([nv[rows, lanes]] * 2, 0).astype(jnp.float32)
                s = jnp.sum(query * key, axis=1, keepdims=True) * LOG2
                w = jnp.exp2(s if j == 0 else jnp.where(step, s, NEG))
                total = total + w
                acc = acc + w.astype(jnp.bfloat16).astype(jnp.float32) * value
            rows = slice(g * 64, g * 64 + 64)
            dp[head, rows, :] = acc
            dl[head, rows, :] = jnp.broadcast_to(total / HD, (64, HD))

    def finish_prompt(head):
        out = sp[head] / jnp.sum(sl[head], axis=0, keepdims=True)
        for g in range(8):
            lanes = slice((head * 8 + g) * HD, (head * 8 + g + 1) * HD)
            part = jnp.transpose(out[:, g * TOK : (g + 1) * TOK])
            pout[:, lanes] = part.astype(jnp.bfloat16)

    def finish_decode(head):
        for g in range(8):
            lanes = slice((head * 8 + g) * HD, (head * 8 + g + 1) * HD)
            rows = slice(g * 64, (g + 1) * 64)
            total = jnp.sum(dl[head, rows, :], axis=1, keepdims=True)
            dout[:, lanes] = (dp[head, rows, :] / total).astype(jnp.bfloat16)

    stores = []

    def settle(head, which):
        if last:
            (finish_decode if which else finish_prompt)(head)
            return
        for i in range(2 * which, 2 * which + 2):
            copy = pltpu.make_async_copy(
                accs[i].at[head], accs_out[i].at[head], out_sem.at[head, i]
            )
            copy.start()
            stores.append(copy)

    def loop(count, work):
        def one(i, _):
            work(i)
            return 0

        lax.fori_loop(0, count, one, 0)

    def when(condition, work):
        if condition is True:
            work()
        elif condition is not False:
            pl.when(condition)(work)

    def tiles(r):
        return 2 if r == 0 or len(sides) == 2 else 1

    for r in (1, 2, 0):
        for copy in needed[r]:
            copy.wait()
        if first:
            own_block(r)
        else:
            for i in range(2):
                acc_loads[r, i].wait()
        if r != 0 or prompt_usable:
            loop(tiles(r), lambda i, r=r: prompt_tile(r, *main_tile(r, i, True)))
        settle(r, 0)
    if first:
        own_block(3)
    else:
        for i in range(2):
            acc_loads[3, i].wait()
    for r in (1, 2, 0):
        if r != 0 or prompt_usable:
            prompt_tile(3, *third_tile(r, 0, True))
    settle(3, 0)

    @pl.when(jnp.logical_not(same))
    def _():
        for copy in others:
            copy.wait()

    for r in (1, 2, 0):
        hand(r, lambda copy: copy.start())
    for r in (1, 2, 0):
        if first:
            fresh(r)
        else:
            for i in range(2, 4):
                acc_loads[r, i].wait()
        when(
            True if r else usable,
            lambda r=r: loop(
                tiles(r), lambda i: decode_tile(r, *main_tile(r, i, same))
            ),
        )
        settle(r, 1)
    if first:
        fresh(3)
    else:
        for i in range(2, 4):
            acc_loads[3, i].wait()
    for r in (1, 2, 0):
        when(
            True if r else usable, lambda r=r: decode_tile(3, *third_tile(r, 0, same))
        )
    settle(3, 1)

    high = jnp.zeros((16, 256), jnp.float32)
    for side, copy in zip(sides, spares):
        copy.wait()
        part = spare[side].reshape(16, 16, 256).astype(jnp.float32)
        high = jnp.maximum(high, jnp.max(part, axis=0))
    mx[...] = high
    for copy in stores:
        copy.wait()
    for r in (1, 2, 0):
        hand(r, lambda copy: copy.wait())


def run_stage(t, meta, lens, q, dq, sources, accs, handed, fresh):
    anywhere = pl.BlockSpec(memory_space=pl.ANY)
    vmem = pl.BlockSpec(memory_space=pltpu.VMEM)
    acc_shapes = [
        jax.ShapeDtypeStruct(shape, jnp.float32)
        for shape in ((4, HD, 1024), (4, 8, 1024), (4, 512, HD), (4, 512, HD))
    ]
    handed_shape = jax.ShapeDtypeStruct((2, 8192, 512), jnp.bfloat16)
    mx_shape = jax.ShapeDtypeStruct((16, 256), jnp.float32)
    carried = [] if t == 0 else [*accs, handed]
    new = [*fresh] if t == 0 else []
    at = 4 + len(sources)
    if t == 4:
        outs = [
            jax.ShapeDtypeStruct(q.shape, jnp.bfloat16),
            jax.ShapeDtypeStruct(dq.shape, jnp.bfloat16),
            handed_shape,
            mx_shape,
        ]
        specs = [vmem, vmem, anywhere, vmem]
        alias = {at + 4: 2}
    else:
        outs = [*acc_shapes, handed_shape, mx_shape]
        specs = [anywhere] * 5 + [vmem]
        alias = {} if t == 0 else {at + i: i for i in range(5)}
    work = 16 * HD * len(sources) // 3 * 6144
    return pl.pallas_call(
        functools.partial(stage_kernel, t),
        out_shape=outs,
        in_specs=[pl.BlockSpec(memory_space=pltpu.SMEM), vmem, vmem, vmem]
        + [anywhere] * (len(sources) + len(carried))
        + [vmem] * len(new),
        out_specs=specs,
        input_output_aliases=alias,
        scratch_shapes=[
            pltpu.VMEM((3, 2, 4, 4, ROWS, 256), jnp.bfloat16),
            pltpu.VMEM((2, 4, 4, 16, 256), jnp.bfloat16),
            pltpu.VMEM((4, HD, 1024), jnp.float32),
            pltpu.VMEM((4, 8, 1024), jnp.float32),
            pltpu.VMEM((4, 512, HD), jnp.float32),
            pltpu.VMEM((4, 512, HD), jnp.float32),
            pltpu.SemaphoreType.DMA((3, 2, 3)),
            pltpu.SemaphoreType.DMA((2,)),
            pltpu.SemaphoreType.DMA((4, 4)),
            pltpu.SemaphoreType.DMA((4, 4)),
            pltpu.SemaphoreType.DMA,
        ],
        compiler_params=pltpu.CompilerParams(vmem_limit_bytes=VMEM),
        cost_estimate=pl.CostEstimate(
            flops=work * 512, bytes_accessed=30 << 20, transcendentals=work
        ),
        name=f"stage{t}",
    )(meta, lens, q, dq, *sources, *carried, *new)


def careful(queries, keys, values, handed, dec_queries, new_keys, new_values, row_len):
    place = lax.axis_index("blk")
    tok, block = TOK, 512
    count = lax.axis_size("blk")
    seq = count * tok
    right = [(i, (i + 1) % count) for i in range(count)]

    def collect(i, carry):
        shard, cache = carry
        cache = lax.dynamic_update_slice(cache, shard, (0, (place - i) % count * tok, 0))
        return lax.ppermute(shard, "blk", right), cache

    shard = jnp.stack([keys[0], values[0]])
    cache = jnp.zeros((2, seq, 512), jnp.bfloat16)
    _, cache = lax.fori_loop(0, count, collect, (shard, cache))
    all_k = cache[0].reshape(seq, 4, HD)
    all_v = cache[1].reshape(seq, 4, HD)

    def attend(query, cache_k, cache_v, limit, state):
        def turn(i, state):
            big, total, acc = state
            part_k = lax.dynamic_slice_in_dim(cache_k, i * block, block, 0)
            part_v = lax.dynamic_slice_in_dim(cache_v, i * block, block, 0)
            s = jnp.einsum("tkgd,skd->kgts", query, part_k, preferred_element_type=jnp.float32)
            s = s * SCALE
            allow = (i * block + jnp.arange(block))[None, :] < limit[:, None]
            s = jnp.where(allow, s, NEG)
            top = jnp.maximum(big, jnp.max(s, axis=-1))
            w = jnp.where(allow, jnp.exp(s - top[..., None]), 0.0)
            shrink = jnp.exp(big - top)
            total = total * shrink + jnp.sum(w, axis=-1)
            acc = acc * shrink[..., None] + jnp.einsum(
                "kgts,skd->kgtd",
                w.astype(jnp.bfloat16),
                part_v,
                preferred_element_type=jnp.float32,
            )
            return top, total, acc

        return lax.fori_loop(0, seq // block, turn, state)

    def finish(state, rows):
        out = state[2] / state[1][..., None]
        return out.transpose(2, 0, 1, 3).reshape(rows, 4096).astype(jnp.bfloat16)

    state = (
        jnp.full((4, 8, tok), NEG, jnp.float32),
        jnp.zeros((4, 8, tok), jnp.float32),
        jnp.zeros((4, 8, tok, HD), jnp.float32),
    )
    limit = place * tok + jnp.arange(tok) + 1
    state = attend(queries[0].reshape(tok, 4, 8, HD), all_k, all_v, limit, state)
    prompt_out = finish(state, tok)

    steps, rows = dec_queries.shape[:2]
    cache_k = handed[0].reshape(seq, 4, HD)
    cache_v = handed[1].reshape(seq, 4, HD)
    outs = []
    for step in range(steps):
        dquery = dec_queries[step].reshape(rows, 4, 8, HD)
        nk = new_keys[: step + 1].reshape(step + 1, rows, 4, HD)
        nv = new_values[: step + 1].reshape(step + 1, rows, 4, HD)
        s = jnp.einsum("rkgd,jrkd->kgrj", dquery, nk, preferred_element_type=jnp.float32) * SCALE
        top = jnp.max(s, axis=-1)
        w = jnp.exp(s - top[..., None])
        acc = jnp.einsum(
            "kgrj,jrkd->kgrd", w.astype(jnp.bfloat16), nv, preferred_element_type=jnp.float32
        )
        state = attend(dquery, cache_k, cache_v, row_len, (top, jnp.sum(w, axis=-1), acc))
        outs.append(finish(state, rows))
    return prompt_out, jnp.stack(outs)


def body(queries, keys, values, match, dec_queries, new_keys, new_values, row_len):
    flat = lax.axis_index("loop") * 64 + lax.axis_index("blk")
    core, y, x = flat % 2, flat // 2 % 4, flat // 8 % 4
    z = flat // 32 % 2 * 2 + flat // 64
    meta = jnp.stack([x, y, z, core, match[0], 0, 0, 0]).astype(jnp.int32)
    q, dq = queries[0], dec_queries.reshape(64, 4096)
    lens = jnp.broadcast_to(jnp.tile(row_len, 2)[:, None], (64, HD)).astype(jnp.int32)
    fresh = [v.reshape(64, 512) for v in (new_keys, new_values)]

    pieces = pack(keys[0], values[0], q, dq, fresh[0])
    pieces = tied([p[None, None] for p in pieces])
    for phase in range(2):
        for step in range(2):
            got = [
                moved(p, rot[phase], lambda a, c: a ^ (1 if step == c else 3))
                for p, rot in zip(pieces, ROTS)
            ]
            got = tied(got)
            axes = [lead if phase == 0 else 1 - lead for lead in LEAD]
            pieces = tied(
                [jnp.concatenate([p, g], a) for p, g, a in zip(pieces, got, axes)]
            )

    accs, handed, sib, high = [], None, [], []
    for t in range(5):
        across = [swapped(p) for p in pieces]
        onward = []
        if t < 3:
            across[0], held = tied([across[0], pieces[2]])
            onward = [
                moved(p, rot[2], lambda a, c: a + 1 - 2 * c)
                for p, rot in zip([pieces[0], pieces[1], held], ROTS)
            ]
        res = run_stage(t, meta, lens, q, dq, [*pieces, *sib], accs, handed, fresh)
        if t < 4:
            accs, handed = res[:4], res[4]
            ready = tied([*onward, *across, *accs, handed])
            pieces, ready = ready[: len(onward)], ready[len(onward) :]
            sib, accs, handed = ready[:3], ready[3:7], ready[7]
        else:
            prompt_out, dec_out, handed = res[:3]
        high.append(res[-1])
    high = functools.reduce(jnp.maximum, high)
    bound = jnp.max(high[:, :HD]) * jnp.max(high[:, HD:]) * LOG2
    prompt_out, dec_out = lax.cond(
        bound < LIMIT,
        lambda: (prompt_out, dec_out.reshape(dec_queries.shape)),
        lambda: careful(
            queries, keys, values, handed, dec_queries, new_keys, new_values, row_len
        ),
    )
    return prompt_out[None], handed[None], dec_out


def solution(mesh):
    in_specs = (
        P("loop", "blk", None),
        P("loop", "blk", None),
        P("loop", "blk", None),
        P(("loop", "blk")),
        P(None, ("loop", "blk"), None),
        P(None, ("loop", "blk"), None),
        P(None, ("loop", "blk"), None),
        P(("loop", "blk")),
    )
    out_specs = (
        P("loop", "blk", None),
        P(("loop", "blk"), None, None, None),
        P(None, ("loop", "blk"), None),
    )
    return jax.shard_map(body, mesh=mesh, in_specs=in_specs, out_specs=out_specs, check_vma=False)
```

```python
import functools
import math

import jax
import jax.numpy as jnp
from jax import lax
from jax.experimental import pallas as pl
from jax.experimental.pallas import tpu as pltpu
from jax.sharding import PartitionSpec as P

HD = 128
TOK = 128
SEG = 48
ROWS = TOK + SEG
AX = ("loop", "blk")
ROTS = ("xyz", "yzx", "zxy")
LEAD = (0, 1, 0)
SCALE = 1.0 / math.sqrt(HD)
LOG2 = math.log2(math.e) * SCALE
NEG = -1e30
BIG = 1 << 30
LIMIT = 100.0
VMEM = 48 * 2**20


def index(x, y, z, c):
    return (z % 2) * 64 + (((z // 2) * 4 + x) * 4 + y) * 2 + c


def moved(value, dim, rule):
    at = "xyz".index(dim)
    route = []
    for flat in range(128):
        c, y, x, z = flat % 2, flat // 2 % 4, flat // 8 % 4, flat // 32
        there = [x, y, z]
        there[at] = rule(there[at], c) % 4
        route.append((index(x, y, z, c), index(*there, c)))
    return lax.ppermute(value, AX, route)


def swapped(value):
    return lax.ppermute(value, AX, [(i, i ^ 1) for i in range(128)])


def tied(values):
    return list(lax.optimization_barrier(tuple(values)))


def dot_nt(a, b):
    return lax.dot_general(a, b, (((1,), (1,)), ((), ())), preferred_element_type=jnp.float32)


def dot_nn(a, b):
    return lax.dot_general(a, b, (((1,), (0,)), ((), ())), preferred_element_type=jnp.float32)


def lane_sums(w):
    total = w[:, :128]
    for at in range(128, w.shape[1], 128):
        total = total + w[:, at : at + 128]
    return total


def positions(bases, n, live):
    it = lax.broadcasted_iota(jnp.int32, (1, len(bases) * n), 1)
    pos = it + bases[0]
    inside = it
    for s in range(1, len(bases)):
        pos = jnp.where(it >= s * n, it + (bases[s] - s * n), pos)
        inside = jnp.where(it >= s * n, it - s * n, inside)
    return jnp.where(inside < live, pos, BIG)


def pack_kernel(keys, values, q, dq, nk, *pieces):
    ones = jnp.ones((HD, HD), jnp.bfloat16)

    def squares(ref):
        best = jnp.zeros((1, HD), jnp.float32)
        for at in range(0, ref.shape[1], HD):
            part = ref[:, at : at + HD].astype(jnp.float32)
            total = dot_nn((part * part).astype(jnp.bfloat16), ones)
            best = jnp.maximum(best, jnp.max(total, axis=0, keepdims=True))
        return best

    for r, piece in enumerate(pieces):
        live = min(SEG, TOK - SEG * r)
        for half, ref in enumerate((keys, values)):
            lanes = slice(half * HD, (half + 1) * HD)
            piece[0:TOK, lanes] = ref[:, r * HD : (r + 1) * HD]
            piece[TOK : TOK + live, lanes] = ref[SEG * r : SEG * r + live, 3 * HD : 4 * HD]
    for half, best in enumerate(
        (jnp.maximum(squares(keys), squares(nk)), jnp.maximum(squares(q), squares(dq)))
    ):
        bound = jnp.broadcast_to(jnp.sqrt(best) * 1.02, (16, HD))
        pieces[2][TOK + 32 : ROWS, half * HD : (half + 1) * HD] = bound.astype(jnp.bfloat16)


def pack(keys, values, q, dq, nk):
    vmem = pl.BlockSpec(memory_space=pltpu.VMEM)
    return pl.pallas_call(
        pack_kernel,
        out_shape=[jax.ShapeDtypeStruct((ROWS, 256), jnp.bfloat16)] * 3,
        in_specs=[vmem] * 5,
        out_specs=[vmem] * 3,
        compiler_params=pltpu.CompilerParams(vmem_limit_bytes=16 * 2**20),
        name="pack",
    )(keys, values, q, dq, nk)


def stage_kernel(t, meta, lens, q, dq, *rest):
    sides = [side for side, on in enumerate((t < 4, t > 0)) if on]
    first, last = t == 0, t == 4
    count = 3 * len(sides)
    sources, rest = rest[:count], rest[count:]
    if first:
        (nk, nv), accs_in, rest = rest[:2], (), rest[2:]
    else:
        accs_in, rest = rest[:4], rest[5:]
    if last:
        (pout, dout, handed, mx), rest = rest[:4], rest[4:]
    else:
        accs_out, handed, mx, rest = rest[:4], rest[4], rest[5], rest[6:]
    buf, spare, sp, sl, dp, dl, load_sem, spare_sem, acc_sem, out_sem, hand_sem = rest
    accs = (sp, sl, dp, dl)
    px, py, pz, core, match = meta[0], meta[1], meta[2], meta[3], meta[4]
    mine = (((pz >> 1) * 4 + px) * 4 + py) * 2 + core
    same = match == (pz & 1)

    near = t % 2
    active = jnp.where(same, near, 1 - near)

    def load(r, side, part):
        source = sources[3 * sides.index(side) + r]
        if part is None:
            return pltpu.make_async_copy(source, buf.at[r, side], load_sem.at[r, side, 0])
        lead, n = ((0, 1), (3, 1), (1, 2))[part]
        span = pl.ds(lead, n)
        return pltpu.make_async_copy(
            source.at[span], buf.at[r, side, span], load_sem.at[r, side, part]
        )

    acc_loads = {
        (head, i): pltpu.make_async_copy(
            accs_in[i].at[head], accs[i].at[head], acc_sem.at[head, i]
        )
        for head in (1, 2, 0, 3)
        for i in range(0 if first else 4)
    }
    needed = {1: [], 2: [], 0: []}
    for r in (1, 2):
        needed[r] = [load(r, side, part) for part in range(2) for side in sides]
    if near in sides:
        needed[0] = [load(0, near, None)]
    others = [load(r, side, 2) for r in (1, 2) for side in sides]
    if 1 - near in sides:
        others.append(load(0, 1 - near, None))
    for r in (1, 2, 0):
        for copy in needed[r]:
            copy.start()
        if not first:
            for i in range(2):
                acc_loads[r, i].start()
    if not first:
        for i in range(2):
            acc_loads[3, i].start()

    @pl.when(jnp.logical_not(same))
    def _():
        for copy in others:
            copy.start()

    spares = [
        pltpu.make_async_copy(
            sources[3 * sides.index(side) + 2].at[:, :, pl.ds(TOK + 32, 16), :],
            spare.at[side],
            spare_sem.at[side],
        )
        for side in sides
    ]
    if not first:
        for head in (1, 2, 0, 3):
            for i in range(2, 4):
                acc_loads[head, i].start()
    for copy in spares:
        copy.start()
    if first:
        sp[...] = jnp.zeros_like(sp)
        sl[...] = jnp.zeros_like(sl)

    def sided(side):
        if isinstance(side, int):
            return (core, t) if side == 0 else (1 - core, t - 1)
        return jnp.where(side == 0, core, 1 - core), jnp.where(side == 0, t, t - 1)

    def place(r, side, lead, inner):
        cs, stage = sided(side)

        def offset(i):
            return jnp.where(
                i == 0, 0, jnp.where(i == 3, 2, jnp.where(i == 1, 1 + 2 * cs, 3 - 2 * cs))
            )

        turn = stage * (2 * cs - 1)
        el, ei = offset(lead), offset(inner)
        x = jnp.where(r == 0, px ^ el, jnp.where(r == 1, (px + turn) & 3, px ^ ei))
        y = jnp.where(r == 2, (py + turn) & 3, py ^ ei)
        z = jnp.where(r == 0, (pz + turn) & 3, pz ^ el)
        return (((z >> 1) * 4 + x) * 4 + y) * 2 + cs

    def facing(lead):
        return jnp.where(lead == 1, 2, jnp.where(lead == 2, 1, lead))

    def led(side, i, own):
        far = 1 + i if side == 0 else 2 - i
        return jnp.where(own, 3 * i, far)

    def hand(r, act):
        live = min(SEG, TOK - SEG * r)

        def slots(side, lead):
            for inner in range(4):
                row = place(r, side, lead, inner) * TOK
                for half in range(2):
                    for lo, n, to, head in ((0, TOK, 0, r), (TOK, live, SEG * r, 3)):
                        act(
                            pltpu.make_async_copy(
                                buf.at[r, side, lead, inner, pl.ds(lo, n), pl.ds(half * HD, HD)],
                                handed.at[
                                    half,
                                    pl.ds(pl.multiple_of(row + to, 16), n),
                                    pl.ds(head * HD, HD),
                                ],
                                hand_sem,
                            )
                        )

        if r == 0:

            def some(i, _):
                slots(active, i)
                return 0

            @pl.when(usable)
            def _():
                lax.fori_loop(0, 4, some, 0)

        else:

            def some(i, _):
                for side in sides:
                    slots(side, led(side, i, same))
                return 0

            lax.fori_loop(0, 2, some, 0)

    usable = True if len(sides) == 2 else active == sides[0]
    prompt_usable = len(sides) == 2 or near == sides[0]

    def gathered(r, groups, lo, n, base, live):
        keys, bases = [], []
        for side, lead in groups:
            keys.append(buf[r, side, lead, :, lo : lo + n, :].reshape(4 * n, 256))
            bases += [place(r, side, lead, inner) * TOK + base for inner in range(4)]
        return jnp.concatenate(keys, 0), bases, n, live

    def groups_of(r, i, own):
        if r == 0:
            side = near if own is True else active
            return [(side, 2 * i), (side, 2 * i + 1)]
        if len(sides) == 2:
            return [(side, led(side, i, own)) for side in sides]
        return [(sides[0], led(sides[0], j, own)) for j in range(2)]

    def main_tile(r, i, own):
        return gathered(r, groups_of(r, i, own), 0, TOK, 0, TOK)

    def whole_tile(r):
        if r == 0:
            groups = [(near, j) for j in range(4)]
        else:
            groups = [(side, led(side, j, True)) for j in range(2) for side in sides]
        return gathered(r, groups, 0, TOK, 0, TOK)

    def third_tile(r, i, own):
        if r == 0:
            side = near if own is True else active
            groups = [(side, j) for j in range(4)]
        else:
            groups = [(side, led(side, j, own)) for j in range(2) for side in sides]
        return gathered(r, groups, TOK, SEG, SEG * r, min(SEG, TOK - SEG * r))

    def queries_of(head):
        return jnp.concatenate(
            [q[:, (head * 8 + g) * HD : (head * 8 + g + 1) * HD] for g in range(8)], 0
        )

    def prompt_add(head, s, v):
        w = jnp.exp2(s)
        sl[head] += jnp.sum(w.reshape(-1, 8, 1024), axis=0)
        sp[head] += dot_nn(jnp.transpose(v), w.astype(jnp.bfloat16))

    def prompt_tile(head, kv, bases, n, live):
        @pl.when(functools.reduce(jnp.minimum, bases) < mine * TOK)
        def _():
            row = lax.broadcasted_iota(jnp.int32, (n, HD), 0)
            lane = lax.broadcasted_iota(jnp.int32, (n, HD), 1)
            hidden = jnp.concatenate(
                [
                    jnp.where(
                        (lane == 0) & ((row >= live) | (base >= mine * TOK)), NEG, 0.0
                    ).astype(jnp.bfloat16)
                    for base in bases
                ],
                0,
            )
            unit = lax.broadcasted_iota(jnp.int32, (1024, HD), 1) == 0
            qs = jnp.concatenate(
                [queries_of(head), unit.astype(jnp.float32).astype(jnp.bfloat16)], 1
            )
            ks = jnp.concatenate([kv[:, :HD], hidden], 1)
            prompt_add(head, dot_nt(ks, qs) * LOG2, kv[:, HD:])

    def decode_tile(head, kv, bases, n, live):
        k, v = kv[:, :HD], kv[:, HD:]
        pos = positions(bases, n, live)
        limit = jnp.concatenate([lens[:, 0:1]] * 4, 0)
        for chunk in range(2):
            rows = slice(chunk * 256, chunk * 256 + 256)
            at = head * 8 + 4 * chunk
            part = [dq[:, g * HD : (g + 1) * HD] for g in range(at, at + 4)]
            s = dot_nt(jnp.concatenate(part, 0), k) * LOG2
            w = jnp.exp2(jnp.where(pos < limit, s, NEG))
            dl[head, rows, :] += lane_sums(w)
            dp[head, rows, :] += dot_nn(w.astype(jnp.bfloat16), v)

    def own_block(head):
        row = lax.broadcasted_iota(jnp.int32, (TOK, 1024), 0)
        col = lax.broadcasted_iota(jnp.int32, (TOK, 1024), 1) % TOK
        if head < 3:
            kv = buf[head, 0, 0, 0, 0:TOK, :]
        else:
            kv = jnp.concatenate(
                [
                    buf[r, 0, 0, 0, TOK : TOK + min(SEG, TOK - SEG * r), :]
                    for r in range(3)
                ],
                0,
            )
        s = dot_nt(kv[:, :HD], queries_of(head)) * LOG2
        prompt_add(head, jnp.where(row <= col, s, NEG), kv[:, HD:])

    def fresh(head):
        lanes = slice(head * HD, (head + 1) * HD)
        step = lax.broadcasted_iota(jnp.int32, (64, 1), 0) >= 32
        for g in range(8):
            at = (head * 8 + g) * HD
            query = dq[:, at : at + HD].astype(jnp.float32)
            acc = total = 0.0
            for j in range(2):
                rows = slice(32 * j, 32 * j + 32)
                key = jnp.concatenate([nk[rows, lanes]] * 2, 0).astype(jnp.float32)
                value = jnp.concatenate([nv[rows, lanes]] * 2, 0).astype(jnp.float32)
                s = jnp.sum(query * key, axis=1, keepdims=True) * LOG2
                w = jnp.exp2(s if j == 0 else jnp.where(step, s, NEG))
                total = total + w
                acc = acc + w.astype(jnp.bfloat16).astype(jnp.float32) * value
            rows = slice(g * 64, g * 64 + 64)
            dp[head, rows, :] = acc
            dl[head, rows, :] = jnp.broadcast_to(total / HD, (64, HD))

    def finish_prompt(head):
        out = sp[head] / jnp.sum(sl[head], axis=0, keepdims=True)
        for g in range(8):
            lanes = slice((head * 8 + g) * HD, (head * 8 + g + 1) * HD)
            part = jnp.transpose(out[:, g * TOK : (g + 1) * TOK])
            pout[:, lanes] = part.astype(jnp.bfloat16)

    def finish_decode(head):
        for g in range(8):
            lanes = slice((head * 8 + g) * HD, (head * 8 + g + 1) * HD)
            rows = slice(g * 64, (g + 1) * 64)
            total = jnp.sum(dl[head, rows, :], axis=1, keepdims=True)
            dout[:, lanes] = (dp[head, rows, :] / total).astype(jnp.bfloat16)

    stores = []

    def settle(head, which):
        if last:
            (finish_decode if which else finish_prompt)(head)
            return
        for i in range(2 * which, 2 * which + 2):
            copy = pltpu.make_async_copy(
                accs[i].at[head], accs_out[i].at[head], out_sem.at[head, i]
            )
            copy.start()
            stores.append(copy)

    def loop(count, work):
        def one(i, _):
            work(i)
            return 0

        lax.fori_loop(0, count, one, 0)

    def when(condition, work):
        if condition is True:
            work()
        elif condition is not False:
            pl.when(condition)(work)

    def tiles(r):
        return 2 if r == 0 or len(sides) == 2 else 1

    for r in (1, 2, 0):
        for copy in needed[r]:
            copy.wait()
        if first:
            own_block(r)
        else:
            for i in range(2):
                acc_loads[r, i].wait()
        if r != 0 or prompt_usable:
            prompt_tile(r, *whole_tile(r))
        settle(r, 0)
    if first:
        own_block(3)
    else:
        for i in range(2):
            acc_loads[3, i].wait()
    for r in (1, 2, 0):
        if r != 0 or prompt_usable:
            prompt_tile(3, *third_tile(r, 0, True))
    settle(3, 0)

    @pl.when(jnp.logical_not(same))
    def _():
        for copy in others:
            copy.wait()

    for r in (1, 2, 0):
        hand(r, lambda copy: copy.start())
    for r in (1, 2, 0):
        if first:
            fresh(r)
        else:
            for i in range(2, 4):
                acc_loads[r, i].wait()
        when(
            True if r else usable,
            lambda r=r: loop(
                tiles(r), lambda i: decode_tile(r, *main_tile(r, i, same))
            ),
        )
        settle(r, 1)
    if first:
        fresh(3)
    else:
        for i in range(2, 4):
            acc_loads[3, i].wait()
    for r in (1, 2, 0):
        when(
            True if r else usable, lambda r=r: decode_tile(3, *third_tile(r, 0, same))
        )
    settle(3, 1)

    high = jnp.zeros((16, 256), jnp.float32)
    for side, copy in zip(sides, spares):
        copy.wait()
        part = spare[side].reshape(16, 16, 256).astype(jnp.float32)
        high = jnp.maximum(high, jnp.max(part, axis=0))
    mx[...] = high
    for copy in stores:
        copy.wait()
    for r in (1, 2, 0):
        hand(r, lambda copy: copy.wait())


def run_stage(t, meta, lens, q, dq, sources, accs, handed, fresh):
    anywhere = pl.BlockSpec(memory_space=pl.ANY)
    vmem = pl.BlockSpec(memory_space=pltpu.VMEM)
    acc_shapes = [
        jax.ShapeDtypeStruct(shape, jnp.float32)
        for shape in ((4, HD, 1024), (4, 8, 1024), (4, 512, HD), (4, 512, HD))
    ]
    handed_shape = jax.ShapeDtypeStruct((2, 8192, 512), jnp.bfloat16)
    mx_shape = jax.ShapeDtypeStruct((16, 256), jnp.float32)
    carried = [] if t == 0 else [*accs, handed]
    new = [*fresh] if t == 0 else []
    at = 4 + len(sources)
    if t == 4:
        outs = [
            jax.ShapeDtypeStruct(q.shape, jnp.bfloat16),
            jax.ShapeDtypeStruct(dq.shape, jnp.bfloat16),
            handed_shape,
            mx_shape,
        ]
        specs = [vmem, vmem, anywhere, vmem]
        alias = {at + 4: 2}
    else:
        outs = [*acc_shapes, handed_shape, mx_shape]
        specs = [anywhere] * 5 + [vmem]
        alias = {} if t == 0 else {at + i: i for i in range(5)}
    work = 16 * HD * len(sources) // 3 * 6144
    return pl.pallas_call(
        functools.partial(stage_kernel, t),
        out_shape=outs,
        in_specs=[pl.BlockSpec(memory_space=pltpu.SMEM), vmem, vmem, vmem]
        + [anywhere] * (len(sources) + len(carried))
        + [vmem] * len(new),
        out_specs=specs,
        input_output_aliases=alias,
        scratch_shapes=[
            pltpu.VMEM((3, 2, 4, 4, ROWS, 256), jnp.bfloat16),
            pltpu.VMEM((2, 4, 4, 16, 256), jnp.bfloat16),
            pltpu.VMEM((4, HD, 1024), jnp.float32),
            pltpu.VMEM((4, 8, 1024), jnp.float32),
            pltpu.VMEM((4, 512, HD), jnp.float32),
            pltpu.VMEM((4, 512, HD), jnp.float32),
            pltpu.SemaphoreType.DMA((3, 2, 3)),
            pltpu.SemaphoreType.DMA((2,)),
            pltpu.SemaphoreType.DMA((4, 4)),
            pltpu.SemaphoreType.DMA((4, 4)),
            pltpu.SemaphoreType.DMA,
        ],
        compiler_params=pltpu.CompilerParams(vmem_limit_bytes=VMEM),
        cost_estimate=pl.CostEstimate(
            flops=work * 512, bytes_accessed=30 << 20, transcendentals=work
        ),
        name=f"stage{t}",
    )(meta, lens, q, dq, *sources, *carried, *new)


def careful(queries, keys, values, handed, dec_queries, new_keys, new_values, row_len):
    place = lax.axis_index("blk")
    tok, block = TOK, 512
    count = lax.axis_size("blk")
    seq = count * tok
    right = [(i, (i + 1) % count) for i in range(count)]

    def collect(i, carry):
        shard, cache = carry
        cache = lax.dynamic_update_slice(cache, shard, (0, (place - i) % count * tok, 0))
        return lax.ppermute(shard, "blk", right), cache

    shard = jnp.stack([keys[0], values[0]])
    cache = jnp.zeros((2, seq, 512), jnp.bfloat16)
    _, cache = lax.fori_loop(0, count, collect, (shard, cache))
    all_k = cache[0].reshape(seq, 4, HD)
    all_v = cache[1].reshape(seq, 4, HD)

    def attend(query, cache_k, cache_v, limit, state):
        def turn(i, state):
            big, total, acc = state
            part_k = lax.dynamic_slice_in_dim(cache_k, i * block, block, 0)
            part_v = lax.dynamic_slice_in_dim(cache_v, i * block, block, 0)
            s = jnp.einsum("tkgd,skd->kgts", query, part_k, preferred_element_type=jnp.float32)
            s = s * SCALE
            allow = (i * block + jnp.arange(block))[None, :] < limit[:, None]
            s = jnp.where(allow, s, NEG)
            top = jnp.maximum(big, jnp.max(s, axis=-1))
            w = jnp.where(allow, jnp.exp(s - top[..., None]), 0.0)
            shrink = jnp.exp(big - top)
            total = total * shrink + jnp.sum(w, axis=-1)
            acc = acc * shrink[..., None] + jnp.einsum(
                "kgts,skd->kgtd",
                w.astype(jnp.bfloat16),
                part_v,
                preferred_element_type=jnp.float32,
            )
            return top, total, acc

        return lax.fori_loop(0, seq // block, turn, state)

    def finish(state, rows):
        out = state[2] / state[1][..., None]
        return out.transpose(2, 0, 1, 3).reshape(rows, 4096).astype(jnp.bfloat16)

    state = (
        jnp.full((4, 8, tok), NEG, jnp.float32),
        jnp.zeros((4, 8, tok), jnp.float32),
        jnp.zeros((4, 8, tok, HD), jnp.float32),
    )
    limit = place * tok + jnp.arange(tok) + 1
    state = attend(queries[0].reshape(tok, 4, 8, HD), all_k, all_v, limit, state)
    prompt_out = finish(state, tok)

    steps, rows = dec_queries.shape[:2]
    cache_k = handed[0].reshape(seq, 4, HD)
    cache_v = handed[1].reshape(seq, 4, HD)
    outs = []
    for step in range(steps):
        dquery = dec_queries[step].reshape(rows, 4, 8, HD)
        nk = new_keys[: step + 1].reshape(step + 1, rows, 4, HD)
        nv = new_values[: step + 1].reshape(step + 1, rows, 4, HD)
        s = jnp.einsum("rkgd,jrkd->kgrj", dquery, nk, preferred_element_type=jnp.float32) * SCALE
        top = jnp.max(s, axis=-1)
        w = jnp.exp(s - top[..., None])
        acc = jnp.einsum(
            "kgrj,jrkd->kgrd", w.astype(jnp.bfloat16), nv, preferred_element_type=jnp.float32
        )
        state = attend(dquery, cache_k, cache_v, row_len, (top, jnp.sum(w, axis=-1), acc))
        outs.append(finish(state, rows))
    return prompt_out, jnp.stack(outs)


def body(queries, keys, values, match, dec_queries, new_keys, new_values, row_len):
    flat = lax.axis_index("loop") * 64 + lax.axis_index("blk")
    core, y, x = flat % 2, flat // 2 % 4, flat // 8 % 4
    z = flat // 32 % 2 * 2 + flat // 64
    meta = jnp.stack([x, y, z, core, match[0], 0, 0, 0]).astype(jnp.int32)
    q, dq = queries[0], dec_queries.reshape(64, 4096)
    lens = jnp.broadcast_to(jnp.tile(row_len, 2)[:, None], (64, HD)).astype(jnp.int32)
    fresh = [v.reshape(64, 512) for v in (new_keys, new_values)]

    pieces = pack(keys[0], values[0], q, dq, fresh[0])
    pieces = tied([p[None, None] for p in pieces])
    for phase in range(2):
        for step in range(2):
            got = [
                moved(p, rot[phase], lambda a, c: a ^ (1 if step == c else 3))
                for p, rot in zip(pieces, ROTS)
            ]
            got = tied(got)
            axes = [lead if phase == 0 else 1 - lead for lead in LEAD]
            pieces = tied(
                [jnp.concatenate([p, g], a) for p, g, a in zip(pieces, got, axes)]
            )

    accs, handed, sib, high = [], None, [], []
    for t in range(5):
        across = [swapped(p) for p in pieces]
        onward = []
        if t < 3:
            across[0], held = tied([across[0], pieces[2]])
            onward = [
                moved(p, rot[2], lambda a, c: a + 1 - 2 * c)
                for p, rot in zip([pieces[0], pieces[1], held], ROTS)
            ]
        res = run_stage(t, meta, lens, q, dq, [*pieces, *sib], accs, handed, fresh)
        if t < 4:
            accs, handed = res[:4], res[4]
            ready = tied([*onward, *across, *accs, handed])
            pieces, ready = ready[: len(onward)], ready[len(onward) :]
            sib, accs, handed = ready[:3], ready[3:7], ready[7]
        else:
            prompt_out, dec_out, handed = res[:3]
        high.append(res[-1])
    high = functools.reduce(jnp.maximum, high)
    bound = jnp.max(high[:, :HD]) * jnp.max(high[:, HD:]) * LOG2
    prompt_out, dec_out = lax.cond(
        bound < LIMIT,
        lambda: (prompt_out, dec_out.reshape(dec_queries.shape)),
        lambda: careful(
            queries, keys, values, handed, dec_queries, new_keys, new_values, row_len
        ),
    )
    return prompt_out[None], handed[None], dec_out


def solution(mesh):
    in_specs = (
        P("loop", "blk", None),
        P("loop", "blk", None),
        P("loop", "blk", None),
        P(("loop", "blk")),
        P(None, ("loop", "blk"), None),
        P(None, ("loop", "blk"), None),
        P(None, ("loop", "blk"), None),
        P(("loop", "blk")),
    )
    out_specs = (
        P("loop", "blk", None),
        P(("loop", "blk"), None, None, None),
        P(None, ("loop", "blk"), None),
    )
    return jax.shard_map(body, mesh=mesh, in_specs=in_specs, out_specs=out_specs, check_vma=False)
```
